32 devices in a mesh: mem: 8 (over z, core), lat: 4 (over y, x).
Axes of the slice: x: 2, y: 2, z: 4, core: 2. Of those that a mesh axis runs over, the one named last changes fastest.
Arguments:
- equivalents: float32 [384, 24576], P('mem', 'lat'), may hold values from -12 to 12
- innovations: float32 [384, 24576], P('mem', 'lat'), may hold values from -6 to 6
- obs_var: float32 [24576], P('lat'), may hold values from 0.5 to 2
- taper_tiles: bfloat16 [2, 512, 512], replicated, may hold values from 0 to 1
- region_blocks: int32 [4, 8], replicated, may hold values from 1 to 2, 12 in all within a row
- pair_mask: int32 [4, 12], replicated, may hold values 0 or 1
- taper_index: int32 [4, 12, 3], replicated, may hold values from 0 to 1
- eig_low: float32 [1], replicated, may hold values from 0.3 to 0.6
- eig_high: float32 [1], replicated, may hold values from 6 to 10
Outputs:
- solution: float32 [384, 24576], P('mem', 'lat')
The draws below stay inside these ranges and needn't reach their ends.
Inputs may be any that keep to these rules, and one draw needn't show every extreme that they name: `region_blocks`: in every band the counts sum to 12 and some region holds exactly 2 blocks.
All inputs are finite; a program needn't handle non-finite values.
Results may differ from the reference program's by a relative error of at most 0.0044.
Values may be sent and summed in bfloat16 or wider, within the bound.
No kernel may reach another device: no remote copies, remote signals or barrier semaphores. Data moves between devices by JAX's collectives and lax.ppermute only.
A program may use at most 64 MiB of HBM per device.

```python
import math
import jax
import jax.numpy as jnp
import numpy as np
from jax import lax

M = 384
BLOCK = 512
MAXB = 2
N_TAPER = 2
ITERS = 3
BAND_BLOCKS = 12
NOBS = 24576
N_MEM = 8
N_LAT = 4


def draw_equivalents(key, part):
    base_key = jax.random.fold_in(key, 4711)
    key_back, key_noise = jax.random.split(base_key, 2)
    background = 4.0 * jax.random.normal(key_back, (1, NOBS), jnp.float32)
    noise = jax.random.normal(key_noise, (M, NOBS), jnp.float32)
    return jnp.clip(background + noise, -12.0, 12.0).astype(jnp.float32)


def touch_ends(entries, stream_key, least, largest):
    longest = entries.shape.index(max(entries.shape))
    spots = []
    for shift in (0, 1):
        where = [jax.random.randint(jax.random.fold_in(stream_key, axis), (), 0, length) for axis, length in enumerate(entries.shape)]
        where[longest] = (where[longest] + shift) % entries.shape[longest]
        spots.append(tuple(where))
    return entries.at[spots[0]].set(least).at[spots[1]].set(largest)


def levels(rng, dims, pieces, smallest, high):
    gain = 1.0
    for position, shards_of in pieces:
        steps = jax.random.uniform(jax.random.fold_in(jax.random.fold_in(rng, 6), position), (shards_of,), jnp.float32, smallest / len(pieces), high / len(pieces))
        gain = gain * jnp.repeat(jnp.exp(steps), dims[position] // shards_of).reshape((-1,) + (1,) * (len(dims) - 1 - position))
    return gain


def length_profile(amount, total, limit, slope):
    loads = [(1 << 20) // math.isqrt(standing ** slope) + 1 for standing in range(2, amount + 1)]
    spare, given = total - limit - (amount - 1), [1] * (amount - 1)
    while spare > 0:
        free = [i for i in range(amount - 1) if given[i] < limit]
        mass, left = sum([loads[i] for i in free]), spare
        for i in free:
            extra = min(limit - given[i], max(1, left * loads[i] // mass), spare)
            given[i] = given[i] + extra
            spare = spare - extra
    return np.array([limit] + given)


def ragged(stream_key, count, total, bound, skew):
    if count == 2:
        one = jax.random.randint(stream_key, (), max(1, total - bound), min(bound, total - 1) + 1)
        return jnp.stack([one, total - one])
    lengths = jnp.asarray(length_profile(count, total, bound, skew), jnp.int32)
    couples = (count - 1) // 2
    source_of, receiver = lengths[1:1 + 2 * couples:2], lengths[2:2 + 2 * couples:2]
    slack = jnp.minimum(source_of - 1, bound - receiver)
    passed = jax.random.randint(jax.random.fold_in(stream_key, 1), (couples,), 0, 1 << 20) % (slack + 1)
    lengths = lengths.at[1:1 + 2 * couples:2].set(source_of - passed).at[2:2 + 2 * couples:2].set(receiver + passed)
    return lengths[jax.random.permutation(jax.random.fold_in(stream_key, 2), count)]


def centred(own_key, shape, spread, reach, pieces=(), kind=jnp.bfloat16):
    values = spread * jax.random.normal(own_key, shape, jnp.float32)
    if pieces:
        values = values * levels(own_key, shape, pieces, -0.22, 0.18)
    return jnp.clip(values, -reach, reach).astype(kind)


def setup_inputs(seed: int = 0) -> dict:
    seeds = jax.random.split(jax.random.key(seed), 10)
    return {
        "equivalents": draw_equivalents(jax.random.fold_in(seeds[9], 71), 0),
        "innovations": centred(seeds[1], (M, NOBS), 1.0, 6.0, ((0, 8), (1, 4)), jnp.float32),
        "obs_var": jnp.clip(jnp.exp(math.log(2.0) - 1.3862944 * jax.random.uniform(seeds[2], (NOBS,), jnp.float32) ** levels(seeds[2], (NOBS,), ((0, 4),), -0.2, 0.2)), 0.5, 2.0),
        "taper_tiles": jnp.clip(jax.random.uniform(seeds[3], (N_TAPER, BLOCK, BLOCK), jnp.float32, 0.0, 1.0), 0.0, 1.0).astype(jnp.bfloat16),
        "region_blocks": jax.vmap(lambda own: ragged(own, N_MEM, BAND_BLOCKS, MAXB, 2))(jax.random.split(seeds[4], N_LAT)).reshape((N_LAT, N_MEM)).astype(jnp.int32),
        "pair_mask": touch_ends((jax.random.randint(seeds[5], (N_LAT, BAND_BLOCKS), 0, 4) < 3).astype(jnp.int32), jax.random.fold_in(seeds[5], 1), 0, 1),
        "taper_index": touch_ends(jax.random.randint(seeds[6], (N_LAT, BAND_BLOCKS, 3), 0, N_TAPER), jax.random.fold_in(seeds[6], 1), 0, N_TAPER - 1).astype(jnp.int32),
        "eig_low": jnp.clip(jax.random.uniform(seeds[7], (1,), jnp.float32, 0.3, 0.6), 0.3, 0.6),
        "eig_high": jnp.clip(jax.random.uniform(seeds[8], (1,), jnp.float32, 6.0, 10.0), 6.0, 10.0),
    }


exact_precision = lax.Precision.HIGHEST


def exclusive_starts(counts):
    return (jnp.cumsum(counts, axis=1) - counts).astype(jnp.int32)


def reference(equivalents, innovations, obs_var, taper_tiles, region_blocks, pair_mask, taper_index, eig_low, eig_high):
    inv_scale = (M - 1) ** -0.5
    ens_blocks = equivalents.T.reshape(N_LAT, BAND_BLOCKS, BLOCK, M)
    mean_rows = jnp.mean(ens_blocks, axis=3, keepdims=True)
    perturb = ((ens_blocks - mean_rows) * inv_scale).astype(jnp.bfloat16)
    starts = exclusive_starts(region_blocks)
    positions = jnp.arange(BAND_BLOCKS, dtype=jnp.int32)
    is_start = jnp.any(positions[None, :, None] == starts[:, None, :], axis=2)
    next_start = jnp.concatenate([is_start[:, 1:], jnp.ones((N_LAT, 1), dtype=jnp.bool_)], axis=1)
    active = ((pair_mask == 1) & jnp.logical_not(next_start)).astype(jnp.float32)
    taper_table = taper_tiles.astype(jnp.float32)

    def band_cov(inputs):
        pert_band, index_band, active_band = inputs
        pert_f32 = pert_band.astype(jnp.float32)
        following = jnp.concatenate([pert_f32[1:], jnp.zeros_like(pert_f32[:1])], axis=0)
        tile_self = taper_table[index_band[:, 0]]
        tile_self = 0.5 * (tile_self + jnp.swapaxes(tile_self, 1, 2))
        prod_self = jnp.einsum("kim,kjm->kij", pert_f32, pert_f32, precision=exact_precision)
        cov_self = (tile_self * prod_self).astype(jnp.bfloat16)
        tile_east = taper_table[index_band[:, 1]]
        prod_east = jnp.einsum("kim,kjm->kij", pert_f32, following, precision=exact_precision)
        cov_east = (tile_east * prod_east * active_band[:, None, None]).astype(jnp.bfloat16)
        return cov_self, cov_east

    cov_self, cov_east = lax.map(band_cov, (perturb, taper_index, active))
    band_rows = jnp.arange(N_LAT, dtype=jnp.int32)[:, None]
    first_pert = perturb[band_rows, starts]
    north_index = taper_index[band_rows, starts, 2]

    def north_cov(inputs):
        lower_first, upper_first, index_row = inputs
        product = jnp.einsum("nim,njm->nij", lower_first.astype(jnp.float32), upper_first.astype(jnp.float32), precision=exact_precision)
        return (taper_table[index_row] * product).astype(jnp.bfloat16)

    cov_north = lax.map(north_cov, (first_pert[:-1], first_pert[1:], north_index[:-1]))
    variance = obs_var.reshape(N_LAT, BAND_BLOCKS, BLOCK, 1)

    def band_apply(inputs):
        self_blocks, east_blocks, dir_band = inputs
        dir_f32 = dir_band.astype(jnp.float32)
        following = jnp.concatenate([dir_f32[1:], jnp.zeros_like(dir_f32[:1])], axis=0)
        before = jnp.concatenate([jnp.zeros_like(dir_f32[:1]), dir_f32[:-1]], axis=0)
        east_f32 = east_blocks.astype(jnp.float32)
        east_prev = jnp.concatenate([jnp.zeros_like(east_f32[:1]), east_f32[:-1]], axis=0)
        summed = jnp.einsum("kij,kjm->kim", self_blocks.astype(jnp.float32), dir_f32, precision=exact_precision)
        summed = summed + jnp.einsum("kij,kjm->kim", east_f32, following, precision=exact_precision)
        return summed + jnp.einsum("kji,kjm->kim", east_prev, before, precision=exact_precision)

    def edge_apply(inputs):
        cov_block, lower_first, upper_first = inputs
        cov_f32 = cov_block.astype(jnp.float32)
        upward = jnp.einsum("nij,njm->nim", cov_f32, upper_first, precision=exact_precision)
        downward = jnp.einsum("nji,njm->nim", cov_f32, lower_first, precision=exact_precision)
        return upward, downward

    def operate(direction):
        dir_bf = direction.astype(jnp.bfloat16)
        result = variance * direction + lax.map(band_apply, (cov_self, cov_east, dir_bf))
        first_dir = dir_bf[band_rows, starts].astype(jnp.float32)
        upward, downward = lax.map(edge_apply, (cov_north, first_dir[:-1], first_dir[1:]))
        zero_band = jnp.zeros_like(upward[:1])
        edge_sum = jnp.concatenate([upward, zero_band], axis=0) + jnp.concatenate([zero_band, downward], axis=0)
        return result.at[band_rows, starts].add(edge_sum)

    low_bound = eig_low[0]
    high_bound = eig_high[0]
    centre = 0.5 * (high_bound + low_bound)
    half_width = 0.5 * (high_bound - low_bound)
    ratio_scale = centre / half_width
    ratio_prev = 1.0 / ratio_scale
    residual = innovations.T.reshape(N_LAT, BAND_BLOCKS, BLOCK, M)
    solution = jnp.zeros_like(residual)
    direction = residual / centre
    for iteration in range(ITERS):
        solution = solution + direction
        if iteration + 1 < ITERS:
            residual = residual - operate(direction)
            ratio_next = 1.0 / (2.0 * ratio_scale - ratio_prev)
            direction = ratio_next * ratio_prev * direction + (2.0 * ratio_next / half_width) * residual
            ratio_prev = ratio_next
    return solution.reshape(N_LAT * BAND_BLOCKS * BLOCK, M).T
```

```python
import functools

import jax
import jax.numpy as jnp
from jax import lax
from jax.experimental import pallas as pl
from jax.experimental.pallas import tpu as pltpu
from jax.sharding import PartitionSpec as P

BF = jnp.bfloat16
F32 = jnp.float32
VMEM_LIMIT = 48 * 1024 * 1024

SMEM_SPEC = pl.BlockSpec(memory_space=pltpu.SMEM)
VMEM_SPEC = pl.BlockSpec(memory_space=pltpu.VMEM)


def kernel_call(body, outs, scalars, arrays, scratch=(), name=None):
    return pl.pallas_call(
        body,
        out_shape=tuple(jax.ShapeDtypeStruct(s, d) for s, d in outs),
        in_specs=[SMEM_SPEC] * len(scalars) + [VMEM_SPEC] * len(arrays),
        out_specs=tuple(VMEM_SPEC for _ in outs),
        scratch_shapes=list(scratch),
        compiler_params=pltpu.CompilerParams(vmem_limit_bytes=VMEM_LIMIT),
        name=name,
    )(*scalars, *arrays)


def dot_nn(a, b):
    return lax.dot_general(a, b, (((1,), (0,)), ((), ())), preferred_element_type=F32)


def dot_nt(a, b):
    return lax.dot_general(a, b, (((1,), (1,)), ((), ())), preferred_element_type=F32)


def dot_tn(a, b):
    return lax.dot_general(a, b, (((0,), (0,)), ((), ())), preferred_element_type=F32)


def region_start(rb, band, m):
    return lax.fori_loop(0, m, lambda i, acc: acc + rb[band, i], jnp.int32(0))


def block_cols(block, width):
    return pl.ds(pl.multiple_of(block * width, width), width)


def chebyshev(low, high, width):
    low = jnp.full((1, width), low, F32)
    high = jnp.full((1, width), high, F32)
    centre = 0.5 * (high + low)
    half = 0.5 * (high - low)
    s = centre / half
    q0 = 1.0 / s
    q1 = 1.0 / (2.0 * s - q0)
    q2 = 1.0 / (2.0 * s - q1)
    inv_c = 1.0 / centre
    keep1, gain1 = q1 * q0, 2.0 * q1 / half
    keep2, gain2 = q2 * q1, 2.0 * q2 / half
    return inv_c, keep1, gain1, keep2, gain2


def on_device(
    equivalents,
    innovations,
    obs_var,
    taper_tiles,
    region_blocks,
    pair_mask,
    taper_index,
    eig_low,
    eig_high,
):
    n = lax.axis_size("mem")
    n_lat = lax.axis_size("lat")
    chips = n // 2
    rows, cols = equivalents.shape
    B = taper_tiles.shape[1]
    nb = cols // B
    members = rows * n
    inv_scale = (members - 1) ** (-0.5)
    rp = -(-rows // 16) * 16
    mp = rp * n
    half = mp // 2

    def put_rows(ref_set, lo, value):
        ref_set(slice(lo, lo + rows), value)
        if rp > rows:
            ref_set(slice(lo + rows, lo + rp), jnp.zeros((rp - rows, B), value.dtype))

    def pack_body(rb, eq, inn, lsum, r1own, r1oth, r2own, r2oth, xoth):
        me, band = lax.axis_index("mem"), lax.axis_index("lat")
        lsum[...] = jnp.sum(eq[...], axis=0, keepdims=True)
        for k in range(chips):
            first = region_start(rb, band, me ^ (2 * k))
            second = jnp.minimum(first + 1, nb - 1)
            put_rows(lambda s, v: r1own.__setitem__((k, s), v), 0, inn[:, block_cols(first, B)].astype(BF))
            put_rows(lambda s, v: r2own.__setitem__((k, s), v), 0, inn[:, block_cols(second, B)].astype(BF))
            first = region_start(rb, band, me ^ (2 * k + 1))
            second = jnp.minimum(first + 1, nb - 1)
            put_rows(lambda s, v: r1oth.__setitem__((k, s), v), 0, inn[:, block_cols(first, B)].astype(BF))
            put_rows(lambda s, v: r2oth.__setitem__((k, s), v), 0, inn[:, block_cols(second, B)].astype(BF))
            put_rows(lambda s, v: xoth.__setitem__((k, s), v), 0, eq[:, block_cols(first, B)])
            put_rows(lambda s, v: xoth.__setitem__((chips + k, s), v), 0, eq[:, block_cols(second, B)])

    slots = (chips, rp, B)
    lsum, r1own, r1oth, r2own, r2oth, xoth = kernel_call(
        pack_body,
        [((1, cols), F32), (slots, BF), (slots, BF), (slots, BF), (slots, BF), ((2 * chips, rp, B), F32)],
        [region_blocks],
        [equivalents, innovations],
        name="pack",
    )
    core_pairs = [(i, i ^ 1) for i in range(n)]

    def swap_core(x):
        return lax.ppermute(x, "mem", core_pairs)

    def z_exchange(parts):
        got = [parts[0]] + [None] * (chips - 1)
        for k in reversed(range(1, chips)):
            got[k] = lax.ppermute(parts[k], "mem", [(i, i ^ (2 * k)) for i in range(n)])
        return got

    r1oth = swap_core(r1oth)
    sums = lax.all_gather(lsum, "mem", axis=0, tiled=True)
    xoth = swap_core(xoth)
    r2oth = swap_core(r2oth)

    def join_body(own, oth, *outs):
        for k in range(chips):
            outs[k][0:rp, :] = own[k]
            outs[k][rp : 2 * rp, :] = oth[k]

    r1_parts = kernel_call(
        join_body, [((2 * rp, B), BF)] * chips, [], [r1own, r1oth], name="join_r1"
    )
    r1_got = z_exchange(r1_parts)

    def perturb(x, sums_ref, block):
        mean = jnp.sum(sums_ref[:, block_cols(block, B)], axis=0, keepdims=True) * (1.0 / members)
        return ((x - mean) * inv_scale).astype(BF)

    def perturb1_body(rb, eq, sums_ref, xo, *outs):
        me, band = lax.axis_index("mem"), lax.axis_index("lat")
        for k in range(chips):
            first = region_start(rb, band, me ^ (2 * k))
            own = perturb(eq[:, block_cols(first, B)], sums_ref, first)
            oth = perturb(xo[k, 0:rows, :], sums_ref, first)
            put = lambda s, v: outs[k].__setitem__((s,), v)
            put_rows(put, 0, own)
            put_rows(put, rp, oth)

    def perturb2_body(rb, eq, sums_ref, xo, r2w, r2o, *outs):
        me, band = lax.axis_index("mem"), lax.axis_index("lat")
        for k in range(chips):
            second = jnp.minimum(region_start(rb, band, me ^ (2 * k)) + 1, nb - 1)
            own = perturb(eq[:, block_cols(second, B)], sums_ref, second)
            oth = perturb(xo[chips + k, 0:rows, :], sums_ref, second)
            put = lambda s, v: outs[k].__setitem__((s,), v)
            put_rows(put, 0, own)
            put_rows(put, rp, oth)
            outs[k][2 * rp : 3 * rp, :] = r2w[k]
            outs[k][3 * rp : 4 * rp, :] = r2o[k]

    p1_parts = kernel_call(
        perturb1_body,
        [((2 * rp, B), BF)] * chips,
        [region_blocks],
        [equivalents, sums, xoth],
        name="perturb_first",
    )
    p1_got = z_exchange(p1_parts)
    p2_parts = kernel_call(
        perturb2_body,
        [((4 * rp, B), BF)] * chips,
        [region_blocks],
        [equivalents, sums, xoth, r2own, r2oth],
        name="perturb_second",
    )
    p2_got = z_exchange(p2_parts)

    pair_list = [(i, i ^ 1) for i in range(n_lat)]
    skew_list = [(i, i + 1) for i in range(1, n_lat - 1, 2)] + [(i + 1, i) for i in range(1, n_lat - 1, 2)]
    hop1_list = [(i, i + 2) for i in range(1, n_lat - 1, 2)] + [(i, i - 2) for i in range(2, n_lat, 2)]
    hop2_list = [(i + 2, i + 1) for i in range(1, n_lat - 1, 2)] + [(i - 2, i - 1) for i in range(2, n_lat, 2)]

    def lat_exchange(whole, low, high):
        relay = lax.ppermute(high, "lat", hop1_list)
        skew_low = lax.ppermute(low, "lat", skew_list)
        pair = lax.ppermute(whole, "lat", pair_list)
        skew_high = lax.ppermute(relay, "lat", hop2_list)
        return pair, skew_low, skew_high

    def gather_body(*refs):
        parts, (whole, low, high) = refs[:chips], refs[chips:]
        step = 2 * rp
        for k in range(chips):
            value = parts[k][...]
            whole[k * step : (k + 1) * step, :] = value
            if k < chips // 2:
                low[k * step : (k + 1) * step, :] = value
            else:
                high[(k - chips // 2) * step : (k + 1 - chips // 2) * step, :] = value

    block_outs = [((mp, B), BF), ((half, B), BF), ((half, B), BF)]
    r1, r1_low, r1_high = kernel_call(gather_body, block_outs, [], r1_got, name="gather_r1")
    r1_pair, r1_skew_low, r1_skew_high = lat_exchange(r1, r1_low, r1_high)
    p1, p1_low, p1_high = kernel_call(gather_body, block_outs, [], p1_got, name="gather_p1")
    p1_pair, p1_skew_low, p1_skew_high = lat_exchange(p1, p1_low, p1_high)

    var_row = obs_var.reshape(1, cols)
    step = 2 * rp

    def region_body(rb, pm, ti, el, eh, tt, var, p1_ref, r1_ref, *refs):
        parts = refs[:chips]
        s1, s2, ce, z1, d2b, t2, p2s, r2s = refs[chips:]
        me, band = lax.axis_index("mem"), lax.axis_index("lat")
        first = region_start(rb, band, me)
        second = jnp.minimum(first + 1, nb - 1)
        count = rb[band, me]
        inv_c, keep1, gain1, keep2, gain2 = chebyshev(el[0], eh[0], B)
        for k in range(chips):
            p2s[k * step : (k + 1) * step, :] = parts[k][0:step, :]
            r2s[k * step : (k + 1) * step, :] = parts[k][step : 2 * step, :]
        p1v, p2v, r1v, r2v = p1_ref[...], p2s[...], r1_ref[...], r2s[...]

        def self_cov(pv, block):
            tile = tt[ti[band, block, 0]].astype(F32)
            tile = 0.5 * (tile + tile.T)
            return (tile * dot_tn(pv, pv)).astype(BF)

        s1[...] = self_cov(p1v, first)
        s2[...] = self_cov(p2v, second)
        active = ((count > 1) & (pm[band, first] == 1)).astype(F32)
        tile_east = tt[ti[band, first, 1]].astype(F32) * active
        ce[...] = (tile_east * dot_tn(p1v, p2v)).astype(BF)
        z1[...] = dot_nn(r1v, s1[...]) + dot_nt(r2v, ce[...])
        prod = dot_nn(r2v, s2[...]) + dot_nn(r1v, ce[...])
        var2 = var[:, block_cols(second, B)]
        r2f = r2v.astype(F32)
        d0 = r2f * inv_c
        res = r2f - (var2 * d0 + prod * inv_c)
        d1 = keep1 * d0 + gain1 * res
        d2b[...] = d1.astype(BF)
        t2[...] = (1.0 + keep2) * d1 + gain2 * (res - var2 * d1)

    mat = ((B, B), BF)
    field = ((mp, B), F32)
    s1, s2, ce, z1, d1b_2, t2 = kernel_call(
        region_body,
        [mat, mat, mat, field, ((mp, B), BF), field],
        [region_blocks, pair_mask, taper_index, eig_low, eig_high],
        [taper_tiles, var_row, p1, r1, *p2_got],
        scratch=[pltpu.VMEM((mp, B), BF), pltpu.VMEM((mp, B), BF)],
        name="region_cov",
    )

    def edge_body(
        rb, ti, el, eh, tt, var, p1_ref, pp, pl_lo, pl_hi, r1_ref, rpair, rl_lo, rl_hi, z1_ref,
        qp, qs, d1w, d1l, d1h, t1, pskew, rskew,
    ):
        me, band = lax.axis_index("mem"), lax.axis_index("lat")
        first = region_start(rb, band, me)
        below = jnp.maximum(band - 1, 0)
        first_below = region_start(rb, below, me)
        even = lax.rem(band, 2) == 0
        tile_up = tt[ti[band, first, 2]].astype(F32).T
        tile_down = tt[ti[below, first_below, 2]].astype(F32)
        pskew[0:half, :] = pl_lo[...]
        pskew[half:mp, :] = pl_hi[...]
        rskew[0:half, :] = rl_lo[...]
        rskew[half:mp, :] = rl_hi[...]
        p1v = p1_ref[...]
        qp[...] = (jnp.where(even, tile_up, tile_down) * dot_tn(pp[...], p1v)).astype(BF)
        qs[...] = (jnp.where(even, tile_down, tile_up) * dot_tn(pskew[...], p1v)).astype(BF)
        prod = z1_ref[...] + dot_nn(rpair[...], qp[...]) + dot_nn(rskew[...], qs[...])
        inv_c, keep1, gain1, keep2, gain2 = chebyshev(el[0], eh[0], B)
        var1 = var[:, block_cols(first, B)]
        r1f = r1_ref[...].astype(F32)
        d0 = r1f * inv_c
        res = r1f - (var1 * d0 + prod * inv_c)
        d1 = keep1 * d0 + gain1 * res
        d1b = d1.astype(BF)
        d1w[...] = d1b
        d1l[...] = d1b[0:half, :]
        d1h[...] = d1b[half:mp, :]
        t1[...] = (1.0 + keep2) * d1 + gain2 * (res - var1 * d1)

    qp, qs, d1b_1, d1_low, d1_high, t1 = kernel_call(
        edge_body,
        [mat, mat, *block_outs, field],
        [region_blocks, taper_index, eig_low, eig_high],
        [
            taper_tiles, var_row, p1, p1_pair, p1_skew_low, p1_skew_high,
            r1, r1_pair, r1_skew_low, r1_skew_high, z1,
        ],
        scratch=[pltpu.VMEM((mp, B), BF), pltpu.VMEM((mp, B), BF)],
        name="edge_cov",
    )
    d1_pair, d1_skew_low, d1_skew_high = lat_exchange(d1b_1, d1_low, d1_high)

    def by_member(out, value):
        me = lax.axis_index("mem")
        for j in range(n):
            out[me ^ j] = value[j * rp : (j + 1) * rp, :].astype(BF)

    def inner_body(el, eh, s1_ref, s2_ref, ce_ref, d1_ref, d2_ref, t1_ref, t2_ref, out, w1):
        gain2 = chebyshev(el[0], eh[0], B)[4]
        d1v, d2v, cev = d1_ref[...], d2_ref[...], ce_ref[...]
        by_member(out, t2_ref[...] - gain2 * (dot_nn(d2v, s2_ref[...]) + dot_nn(d1v, cev)))
        w1[...] = t1_ref[...] - gain2 * (dot_nn(d1v, s1_ref[...]) + dot_nt(d2v, cev))

    back = ((n, rp, B), BF)
    sol_2, w1 = kernel_call(
        inner_body,
        [back, field],
        [eig_low, eig_high],
        [s1, s2, ce, d1b_1, d1b_2, t1, t2],
        name="inner_step",
    )

    def outer_body(el, eh, qp_ref, qs_ref, dp, dl, dh, w1_ref, out, dskew):
        gain2 = chebyshev(el[0], eh[0], B)[4]
        dskew[0:half, :] = dl[...]
        dskew[half:mp, :] = dh[...]
        prod = dot_nn(dp[...], qp_ref[...]) + dot_nn(dskew[...], qs_ref[...])
        by_member(out, w1_ref[...] - gain2 * prod)

    (sol_1,) = kernel_call(
        outer_body,
        [back],
        [eig_low, eig_high],
        [qp, qs, d1_pair, d1_skew_low, d1_skew_high, w1],
        scratch=[pltpu.VMEM((mp, B), BF)],
        name="outer_step",
    )
    sol_2 = lax.all_to_all(sol_2, "mem", split_axis=0, concat_axis=0, tiled=True)
    sol_1 = lax.all_to_all(sol_1, "mem", split_axis=0, concat_axis=0, tiled=True)

    def unpack_body(rb, el, eh, inn, a1, a2, out):
        band = lax.axis_index("lat")
        inv_c = chebyshev(el[0], eh[0], B)[0]
        block = jnp.int32(0)
        for m in range(n):
            at = block_cols(block, B)
            out[:, at] = inn[:, at] * inv_c + a1[m, 0:rows, :].astype(F32)
            count = rb[band, m]
            after = block + 1

            @pl.when(count > 1)
            def _():
                at2 = block_cols(jnp.minimum(after, nb - 1), B)
                out[:, at2] = inn[:, at2] * inv_c + a2[m, 0:rows, :].astype(F32)

            block = block + count

    (out,) = kernel_call(
        unpack_body,
        [((rows, cols), F32)],
        [region_blocks, eig_low, eig_high],
        [innovations, sol_1, sol_2],
        name="unpack",
    )
    return out


def solution(mesh):
    return jax.shard_map(
        on_device,
        mesh=mesh,
        in_specs=(P("mem", "lat"), P("mem", "lat"), P("lat"), P(), P(), P(), P(), P(), P()),
        out_specs=P("mem", "lat"),
        check_vma=False,
    )
```

```python
import math

import jax
import jax.numpy as jnp
from jax import lax
from jax.experimental import pallas as pl
from jax.experimental.pallas import tpu as pltpu
from jax.sharding import PartitionSpec as P

BF = jnp.bfloat16
F32 = jnp.float32
VMEM_LIMIT = 12 * 1024 * 1024

SMEM_SPEC = pl.BlockSpec(memory_space=pltpu.SMEM)
VMEM_SPEC = pl.BlockSpec(memory_space=pltpu.VMEM)
ANY_SPEC = pl.BlockSpec(memory_space=pl.ANY)
HBM_SPEC = pl.BlockSpec(memory_space=pltpu.HBM)


def kernel_call(body, outs, scalars, arrays, scratch=(), name=None, array_spec=VMEM_SPEC, after=(), vmem=VMEM_LIMIT):
    used, unread = len(scalars) + len(arrays), len(after)
    moved = sum(a.size * a.dtype.itemsize for a in arrays)
    moved += sum(jnp.dtype(d).itemsize * math.prod(s) for s, d in outs)

    def run(*refs):
        body(*refs[:used], *refs[used + unread :])

    return pl.pallas_call(
        run,
        out_shape=tuple(jax.ShapeDtypeStruct(s, d) for s, d in outs),
        in_specs=[SMEM_SPEC] * len(scalars) + [array_spec] * len(arrays) + [ANY_SPEC] * unread,
        out_specs=tuple(VMEM_SPEC for _ in outs),
        scratch_shapes=list(scratch),
        compiler_params=pltpu.CompilerParams(vmem_limit_bytes=vmem),
        cost_estimate=pl.CostEstimate(flops=3 * 10**9, bytes_accessed=3 * 10**7, transcendentals=0),
        name=name,
    )(*scalars, *arrays, *after)


def gate(x, after):
    def nothing(*refs):
        del refs

    return pl.pallas_call(
        nothing,
        out_shape=jax.ShapeDtypeStruct(x.shape, x.dtype),
        in_specs=[ANY_SPEC] * (1 + len(after)),
        out_specs=ANY_SPEC,
        input_output_aliases={0: 0},
        compiler_params=pltpu.CompilerParams(vmem_limit_bytes=1024 * 1024),
        name="gate",
    )(x, *after)


def dot_nn(a, b):
    return lax.dot_general(a, b, (((1,), (0,)), ((), ())), preferred_element_type=F32)


def dot_nt(a, b):
    return lax.dot_general(a, b, (((1,), (1,)), ((), ())), preferred_element_type=F32)


def dot_tn(a, b):
    return lax.dot_general(a, b, (((0,), (0,)), ((), ())), preferred_element_type=F32)


def region_start(rb, band, m):
    return lax.fori_loop(0, m, lambda i, acc: acc + rb[band, i], jnp.int32(0))


def block_cols(block, width):
    return pl.ds(pl.multiple_of(block * width, width), width)


def chebyshev(low, high, width):
    low = jnp.full((1, width), low, F32)
    high = jnp.full((1, width), high, F32)
    centre = 0.5 * (high + low)
    half = 0.5 * (high - low)
    s = centre / half
    q0 = 1.0 / s
    q1 = 1.0 / (2.0 * s - q0)
    q2 = 1.0 / (2.0 * s - q1)
    inv_c = 1.0 / centre
    keep1, gain1 = q1 * q0, 2.0 * q1 / half
    keep2, gain2 = q2 * q1, 2.0 * q2 / half
    return inv_c, keep1, gain1, keep2, gain2


def on_device(
    equivalents,
    innovations,
    obs_var,
    taper_tiles,
    region_blocks,
    pair_mask,
    taper_index,
    eig_low,
    eig_high,
):
    n = lax.axis_size("mem")
    n_lat = lax.axis_size("lat")
    chips = n // 2
    rows, cols = equivalents.shape
    B = taper_tiles.shape[1]
    nb = cols // B
    members = rows * n
    inv_scale = (members - 1) ** (-0.5)
    rp = -(-rows // 16) * 16
    mp = rp * n
    half = mp // 2

    def put_rows(ref_set, lo, value):
        ref_set(slice(lo, lo + rows), value)
        if rp > rows:
            ref_set(slice(lo + rows, lo + rp), jnp.zeros((rp - rows, B), value.dtype))

    tail_rows = 16
    msg = 2 * rp + tail_rows

    def mean_rows(x, offset):
        mean = jnp.sum(x, axis=0, keepdims=True) * (1.0 / rows)
        high = mean.astype(BF).astype(F32)
        mid = (mean - high).astype(BF).astype(F32)
        row = lax.broadcasted_iota(jnp.int32, (tail_rows, B), 0)
        tail = jnp.where(row == offset + 2, mean - high - mid, 0.0)
        tail = jnp.where(row == offset + 1, mid, tail)
        tail = jnp.where(row == offset, high, tail)
        return mean, tail.astype(BF)

    def blocks(rb, extra):
        me, band = lax.axis_index("mem"), lax.axis_index("lat")
        return [
            block_cols(jnp.minimum(region_start(rb, band, me ^ i) + extra, nb - 1), B) for i in range(n)
        ]

    def fill_p(own, oth, at_row, rb, eq, extra):
        for i, at in enumerate(blocks(rb, extra)):
            k, j = i // 2, i % 2
            out = oth if j else own
            x = eq[:, at]
            mean, tail = mean_rows(x, 8 * j)
            put = lambda s, v: out.__setitem__((k, s), v)
            put_rows(put, at_row, ((x - mean) * inv_scale).astype(BF))
            out[k, at_row + rp : at_row + rp + tail_rows, :] = tail

    def fill_r(own, oth, rb, inn, extra):
        for i, at in enumerate(blocks(rb, extra)):
            out = oth if i % 2 else own
            put_rows(lambda s, v: out.__setitem__((i // 2, s), v), 0, inn[:, at].astype(BF))

    def pack_first_body(rb_hbm, eq_hbm, inn_hbm, own, oth, eq, inn, rb, sems):
        copies = [
            pltpu.make_async_copy(src, dst, sems.at[i])
            for i, (src, dst) in enumerate(((rb_hbm, rb), (inn_hbm, inn), (eq_hbm, eq)))
        ]
        for copy in copies:
            copy.start()
        copies[0].wait()
        copies[1].wait()
        fill_r(own, oth, rb, inn, 0)
        copies[2].wait()
        fill_p(own, oth, rp, rb, eq, 0)

    slot_outs = [((chips, msg, B), BF)] * 2
    own1, oth1 = kernel_call(
        pack_first_body,
        slot_outs,
        [],
        [region_blocks, equivalents, innovations],
        scratch=[
            pltpu.VMEM((rows, cols), F32),
            pltpu.VMEM((rows, cols), F32),
            pltpu.SMEM(region_blocks.shape, jnp.int32),
            pltpu.SemaphoreType.DMA((3,)),
        ],
        name="pack_first",
        array_spec=HBM_SPEC,
        vmem=60 * 1024 * 1024,
    )
    oth1 = lax.ppermute(oth1, "mem", [(i, i ^ 1) for i in range(n)])

    def pack_second_body(rb, eq, inn, own, oth):
        fill_r(own, oth, rb, inn, 1)
        fill_p(own, oth, rp, rb, eq, 1)

    own2, oth2 = kernel_call(
        pack_second_body,
        slot_outs,
        [region_blocks],
        [equivalents, innovations],
        name="pack_second",
        after=[own1],
    )

    core_pairs = [(i, i ^ 1) for i in range(n)]

    def swap_core(x):
        return lax.ppermute(x, "mem", core_pairs)

    def z_exchange(parts, order):
        got = list(parts)
        for k in order:
            got[k] = lax.ppermute(parts[k], "mem", [(i, i ^ (2 * k)) for i in range(n)])
        return got

    far_first = list(range(1, chips))[::-1]
    step = 2 * rp

    def join_body(own, oth, *outs):
        for k in range(chips):
            out = outs[k]
            out[0:rp, :] = own[k, rp:step, :]
            out[rp:step, :] = oth[k, rp:step, :]
            out[step:msg, :] = own[k, step:msg, :] + oth[k, step:msg, :]
            out[msg : msg + rp, :] = own[k, 0:rp, :]
            out[msg + rp : msg + step, :] = oth[k, 0:rp, :]

    def join(own, oth, name, after=()):
        return kernel_call(
            join_body, [((msg + step, B), BF)] * chips, [], [own, oth], name=name, after=after
        )

    m1_got = z_exchange(join(own1, oth1, "join_first"), far_first)
    m2_parts = join(own2, swap_core(oth2), "join_second")
    m2_got = z_exchange(m2_parts, far_first)

    def corrected(pieces):
        mean = sum(m for _, m in pieces) * (1.0 / n)
        out = []
        for x, m in pieces:
            x = x.astype(F32) + (m - mean) * inv_scale
            if rp > rows:
                x = jnp.where(lax.broadcasted_iota(jnp.int32, (rp, B), 0) < rows, x, 0.0)
            out.append(x.astype(BF))
        return out

    odd = range(1, n_lat - 1, 2)
    pair_list = [(i, i ^ 1) for i in range(n_lat)]
    skew_list = [(i, i + 1) for i in odd] + [(i + 1, i) for i in odd]
    hop1_list = [(i, i + 2) for i in odd] + [(i + 1, i - 1) for i in odd]
    hop2_list = [(i + 2, i + 1) for i in odd] + [(i - 1, i) for i in odd]

    def lat_exchange(both, low, high, after=()):
        relay = lax.ppermute(high, "lat", hop1_list)
        pair = lax.ppermute(both, "lat", pair_list)
        skew_low = lax.ppermute(low, "lat", skew_list)
        skew_high = lax.ppermute(gate(relay, after) if after else relay, "lat", hop2_list)
        return pair, skew_low, skew_high

    block_out = ((mp, B), BF)
    half_out = ((half, B), BF)

    def group_rows(part):
        tail = part[step:msg, :].astype(F32)
        return [
            (part[j * rp : (j + 1) * rp, :], jnp.sum(tail[8 * j : 8 * j + 8, :], axis=0, keepdims=True))
            for j in range(2)
        ]

    def owner_body(*refs):
        parts, (both, low, high) = refs[:chips], refs[chips:]

        def put(lo, i, value):
            both[lo * 2 + i * rp : lo * 2 + (i + 1) * rp, :] = value
            out, at = (low, lo + i * rp) if i < chips else (high, lo + (i - chips) * rp)
            out[at : at + rp, :] = value

        for i in range(n):
            at = msg + (i % 2) * rp
            put(half, i, parts[i // 2][at : at + rp, :])
        for i, x in enumerate(corrected([g for part in parts for g in group_rows(part)])):
            put(0, i, x)

    both_out = ((2 * mp, B), BF)
    first, first_low, first_high = kernel_call(
        owner_body, [both_out, block_out, block_out], [], m1_got, name="owner_first", after=[m2_parts[0]]
    )
    pair, skew_low, skew_high = lat_exchange(first, first_low, first_high, after=[m2_got[1]])

    var_row = obs_var.reshape(1, cols)

    def whole(low, high):
        return jnp.concatenate([low[...], high[...]], axis=0)

    mat = ((B, B), BF)
    field = ((mp, B), F32)
    half_field = ((half, B), F32)

    def self_cov(tt, index, pv):
        tile = tt[index].astype(F32)
        tile = 0.5 * (tile + tile.T)
        return (tile * dot_tn(pv, pv)).astype(BF)

    def first_body(rb, ti, tt, first_ref, s1, z1):
        me, band = lax.axis_index("mem"), lax.axis_index("lat")
        first = region_start(rb, band, me)
        s1[...] = self_cov(tt, ti[band, first, 0], first_ref[0:mp, :])
        z1[...] = dot_nn(first_ref[mp:, :], s1[...])

    s1, z1 = kernel_call(
        first_body,
        [mat, field],
        [region_blocks, taper_index],
        [taper_tiles, first],
        name="first_cov",
    )

    def east_body(rb, pm, ti, tt, first_ref, *refs):
        parts, (z1_ref, ce, z1, p2, r2) = refs[:chips], refs[chips:]
        me, band = lax.axis_index("mem"), lax.axis_index("lat")
        first = region_start(rb, band, me)
        for k in range(chips):
            r2[k * step : (k + 1) * step, :] = parts[k][msg : msg + step, :]
        for i, x in enumerate(corrected([g for part in parts for g in group_rows(part)])):
            p2[i * rp : (i + 1) * rp, :] = x
        active = ((rb[band, me] > 1) & (pm[band, first] == 1)).astype(F32)
        tile_east = tt[ti[band, first, 1]].astype(F32) * active
        ce[...] = (tile_east * dot_tn(first_ref[0:mp, :], p2[...])).astype(BF)
        z1[...] = z1_ref[...] + dot_nt(r2[...], ce[...])

    ce, z1, p2, r2 = kernel_call(
        east_body,
        [mat, field, block_out, block_out],
        [region_blocks, pair_mask, taper_index],
        [taper_tiles, first, *m2_got, z1],
        name="east_cov",
    )

    def edge_body(rb, ti, tt, first_ref, pair_ref, sl, sh, qp, qs):
        me, band = lax.axis_index("mem"), lax.axis_index("lat")
        first = region_start(rb, band, me)
        below = jnp.maximum(band - 1, 0)
        first_below = region_start(rb, below, me)
        even = lax.rem(band, 2) == 0
        tile_up = tt[ti[band, first, 2]].astype(F32).T
        tile_down = tt[ti[below, first_below, 2]].astype(F32)
        p1v = first_ref[0:mp, :]
        skew = jnp.concatenate([sl[0:half, :], sh[0:half, :]], axis=0)
        qp[...] = (jnp.where(even, tile_up, tile_down) * dot_tn(pair_ref[0:mp, :], p1v)).astype(BF)
        qs[...] = (jnp.where(even, tile_down, tile_up) * dot_tn(skew, p1v)).astype(BF)

    qp, qs = kernel_call(
        edge_body,
        [mat, mat],
        [region_blocks, taper_index],
        [taper_tiles, first, pair, skew_low, skew_high],
        name="edge_cov",
    )

    def direction_body(rb, el, eh, var, qp_ref, qs_ref, first_ref, pair_ref, sl, sh, z1_ref, d1, d1l, d1h, t1):
        me, band = lax.axis_index("mem"), lax.axis_index("lat")
        first = region_start(rb, band, me)
        inv_c, keep1, gain1, keep2, gain2 = chebyshev(el[0], eh[0], B)
        var1 = var[:, block_cols(first, B)]
        skew = jnp.concatenate([sl[half:, :], sh[half:, :]], axis=0)
        prod = z1_ref[...] + dot_nn(pair_ref[mp:, :], qp_ref[...]) + dot_nn(skew, qs_ref[...])
        r1f = first_ref[mp:, :].astype(F32)
        d0 = r1f * inv_c
        res = r1f - (var1 * d0 + prod * inv_c)
        d = keep1 * d0 + gain1 * res
        db = d.astype(BF)
        d1[...] = db
        d1l[...] = db[0:half, :]
        d1h[...] = db[half:mp, :]
        t1[...] = (1.0 + keep2) * d + gain2 * (res - var1 * d)

    d1, d1_low, d1_high, t1 = kernel_call(
        direction_body,
        [block_out, half_out, half_out, field],
        [region_blocks, eig_low, eig_high],
        [var_row, qp, qs, first, pair, skew_low, skew_high, z1],
        name="direction_first",
    )
    d1_pair, d1_skew_low, d1_skew_high = lat_exchange(d1, d1_low, d1_high)

    def inner_body(
        rb, ti, el, eh, tt, var, p2_ref, r2_ref, first_ref, s1_ref, ce_ref, d1_ref, t1_ref, w1, *outs
    ):
        me, band = lax.axis_index("mem"), lax.axis_index("lat")
        second = jnp.minimum(region_start(rb, band, me) + 1, nb - 1)
        inv_c, keep1, gain1, keep2, gain2 = chebyshev(el[0], eh[0], B)
        d1v, r2v, cev = d1_ref[...], r2_ref[...], ce_ref[...]
        s2 = self_cov(tt, ti[band, second, 0], p2_ref[...])
        prod = dot_nn(r2v, s2) + dot_nn(first_ref[mp:, :], cev)
        var2 = var[:, block_cols(second, B)]
        r2f = r2v.astype(F32)
        d0 = r2f * inv_c
        res = r2f - (var2 * d0 + prod * inv_c)
        d2 = keep1 * d0 + gain1 * res
        d2b = d2.astype(BF)
        w1[...] = t1_ref[...] - gain2 * (dot_nn(d1v, s1_ref[...]) + dot_nt(d2b, cev))
        sol = (1.0 + keep2) * d2 + gain2 * (res - var2 * d2 - dot_nn(d2b, s2) - dot_nn(d1v, cev))
        for k in range(chips):
            outs[k][...] = sol[k * step : (k + 1) * step, :].astype(BF)

    w1, *sol2 = kernel_call(
        inner_body,
        [field] + [((step, B), BF)] * chips,
        [region_blocks, taper_index, eig_low, eig_high],
        [taper_tiles, var_row, p2, r2, first, s1, ce, d1, t1],
        name="inner_step",
    )
    sol2 = z_exchange(sol2, far_first)

    def peer_body(*refs):
        for k in range(chips):
            refs[chips][k] = refs[k][rp:step, :]

    (sol2_peer,) = kernel_call(peer_body, [((chips, rp, B), BF)], [], sol2, name="peer_rows")
    sol2_peer = swap_core(sol2_peer)

    def outer_body(el, eh, qp_ref, qs_ref, dp, dsl, dsh, w1_ref, *outs):
        gain2 = chebyshev(el[0], eh[0], B)[4]
        prod = dot_nn(dp[...], qp_ref[...]) + dot_nn(whole(dsl, dsh), qs_ref[...])
        sol = w1_ref[...] - gain2 * prod
        for i in range(n):
            outs[i][...] = sol[i * rp : (i + 1) * rp, :].astype(BF)

    sol1 = kernel_call(
        outer_body,
        [((rp, B), BF)] * n,
        [eig_low, eig_high],
        [qp, qs, d1_pair, d1_skew_low, d1_skew_high, w1],
        name="outer_step",
        after=sol2[1:],
    )
    sol1 = [
        x if i == 0 else lax.ppermute(x, "mem", [(q, q ^ i) for q in range(n)]) for i, x in enumerate(sol1)
    ]

    def unpack_body(rb, el, eh, inn, *refs):
        firsts, seconds, peer, out = refs[:n], refs[n : n + chips], refs[n + chips], refs[-1]
        me, band = lax.axis_index("mem"), lax.axis_index("lat")
        inv_c = chebyshev(el[0], eh[0], B)[0]
        for i in range(n):
            owner = me ^ i
            first = region_start(rb, band, owner)
            at = block_cols(first, B)
            out[:, at] = inn[:, at] * inv_c + firsts[i][0:rows, :].astype(F32)
            second = jnp.minimum(first + 1, nb - 1)

            @pl.when(rb[band, owner] > 1)
            def _(i=i, second=second):
                at2 = block_cols(second, B)
                add = peer[i // 2, 0:rows, :] if i % 2 else seconds[i // 2][0:rows, :]
                out[:, at2] = inn[:, at2] * inv_c + add.astype(F32)

    (out,) = kernel_call(
        unpack_body,
        [((rows, cols), F32)],
        [region_blocks, eig_low, eig_high],
        [innovations, *sol1, *sol2, sol2_peer],
        name="unpack",
    )
    return out


def solution(mesh):
    return jax.shard_map(
        on_device,
        mesh=mesh,
        in_specs=(P("mem", "lat"), P("mem", "lat"), P("lat"), P(), P(), P(), P(), P(), P()),
        out_specs=P("mem", "lat"),
        check_vma=False,
    )
```

```python
import math

import jax
import jax.numpy as jnp
from jax import lax
from jax.experimental import pallas as pl
from jax.experimental.pallas import tpu as pltpu
from jax.sharding import PartitionSpec as P

BF = jnp.bfloat16
F32 = jnp.float32
VMEM_LIMIT = 12 * 1024 * 1024

SMEM_SPEC = pl.BlockSpec(memory_space=pltpu.SMEM)
VMEM_SPEC = pl.BlockSpec(memory_space=pltpu.VMEM)
ANY_SPEC = pl.BlockSpec(memory_space=pl.ANY)
HBM_SPEC = pl.BlockSpec(memory_space=pltpu.HBM)


def kernel_call(body, outs, scalars, arrays, scratch=(), name=None, array_spec=VMEM_SPEC, after=(), vmem=VMEM_LIMIT):
    used, unread = len(scalars) + len(arrays), len(after)
    moved = sum(a.size * a.dtype.itemsize for a in arrays)
    moved += sum(jnp.dtype(d).itemsize * math.prod(s) for s, d in outs)

    def run(*refs):
        body(*refs[:used], *refs[used + unread :])

    return pl.pallas_call(
        run,
        out_shape=tuple(jax.ShapeDtypeStruct(s, d) for s, d in outs),
        in_specs=[SMEM_SPEC] * len(scalars) + [array_spec] * len(arrays) + [ANY_SPEC] * unread,
        out_specs=tuple(VMEM_SPEC for _ in outs),
        scratch_shapes=list(scratch),
        compiler_params=pltpu.CompilerParams(vmem_limit_bytes=vmem),
        cost_estimate=pl.CostEstimate(flops=3 * 10**9, bytes_accessed=3 * 10**7, transcendentals=0),
        name=name,
    )(*scalars, *arrays, *after)


def gate(x, after):
    def nothing(*refs):
        del refs

    return pl.pallas_call(
        nothing,
        out_shape=jax.ShapeDtypeStruct(x.shape, x.dtype),
        in_specs=[ANY_SPEC] * (1 + len(after)),
        out_specs=ANY_SPEC,
        input_output_aliases={0: 0},
        compiler_params=pltpu.CompilerParams(vmem_limit_bytes=1024 * 1024),
        name="gate",
    )(x, *after)


def dot_nn(a, b):
    return lax.dot_general(a, b, (((1,), (0,)), ((), ())), preferred_element_type=F32)


def dot_nt(a, b):
    return lax.dot_general(a, b, (((1,), (1,)), ((), ())), preferred_element_type=F32)


def dot_tn(a, b):
    return lax.dot_general(a, b, (((0,), (0,)), ((), ())), preferred_element_type=F32)


def region_start(rb, band, m):
    return lax.fori_loop(0, m, lambda i, acc: acc + rb[band, i], jnp.int32(0))


def block_cols(block, width):
    return pl.ds(pl.multiple_of(block * width, width), width)


def chebyshev(low, high, width):
    low = jnp.broadcast_to(low, (8, width))
    high = jnp.broadcast_to(high, (8, width))
    centre = 0.5 * (high + low)
    half = 0.5 * (high - low)
    s = centre / half
    q0 = 1.0 / s
    q1 = 1.0 / (2.0 * s - q0)
    q2 = 1.0 / (2.0 * s - q1)
    row = lax.broadcasted_iota(jnp.int32, (8, width), 0)
    out = 1.0 / centre
    for i, value in enumerate((q1 * q0, 2.0 * q1 / half, q2 * q1, 2.0 * q2 / half)):
        out = jnp.where(row == i + 1, value, out)
    return out


def coefficients(coef):
    return [coef[i : i + 1, :] for i in range(5)]


def on_device(
    equivalents,
    innovations,
    obs_var,
    taper_tiles,
    region_blocks,
    pair_mask,
    taper_index,
    eig_low,
    eig_high,
):
    n = lax.axis_size("mem")
    n_lat = lax.axis_size("lat")
    chips = n // 2
    rows, cols = equivalents.shape
    B = taper_tiles.shape[1]
    nb = cols // B
    members = rows * n
    inv_scale = (members - 1) ** (-0.5)
    rp = -(-rows // 16) * 16
    mp = rp * n
    half = mp // 2

    def put_rows(ref_set, lo, value):
        ref_set(slice(lo, lo + rows), value)
        if rp > rows:
            ref_set(slice(lo + rows, lo + rp), jnp.zeros((rp - rows, B), value.dtype))

    tail_rows = 8
    msg = 2 * rp + tail_rows
    step = 2 * rp

    def mean_rows(x, offset):
        mean = jnp.sum(x, axis=0, keepdims=True) * (1.0 / rows)
        high = mean.astype(BF).astype(F32)
        mid = (mean - high).astype(BF).astype(F32)
        row = lax.broadcasted_iota(jnp.int32, (tail_rows, B), 0)
        tail = jnp.where(row == offset + 2, mean - high - mid, 0.0)
        tail = jnp.where(row == offset + 1, mid, tail)
        tail = jnp.where(row == offset, high, tail)
        return mean, tail.astype(BF)

    def blocks(rb, extra):
        me, band = lax.axis_index("mem"), lax.axis_index("lat")
        return [
            block_cols(jnp.minimum(region_start(rb, band, me ^ i) + extra, nb - 1), B) for i in range(n)
        ]

    def fill_p(own, oth, at_row, rb, eq, extra):
        for i, at in enumerate(blocks(rb, extra)):
            k, j = i // 2, i % 2
            out = oth if j else own
            x = eq[:, at]
            mean, tail = mean_rows(x, 3 * j)
            put = lambda s, v: out.__setitem__((k, s), v)
            put_rows(put, at_row, ((x - mean) * inv_scale).astype(BF))
            out[k, step:msg, :] = tail

    def fill_r(own, oth, rb, inn, extra):
        for i, at in enumerate(blocks(rb, extra)):
            out = oth if i % 2 else own
            put_rows(lambda s, v: out.__setitem__((i // 2, s), v), 0, inn[:, at].astype(BF))

    def pack_body(rb_hbm, eq_hbm, inn_hbm, own1, oth1, own2, oth2, eq, inn, rb, sems):
        copies = [
            pltpu.make_async_copy(src, dst, sems.at[i])
            for i, (src, dst) in enumerate(((rb_hbm, rb), (inn_hbm, inn), (eq_hbm, eq)))
        ]
        for copy in copies:
            copy.start()
        copies[0].wait()
        copies[1].wait()
        fill_r(own1, oth1, rb, inn, 0)
        fill_r(own2, oth2, rb, inn, 1)
        copies[2].wait()
        fill_p(own1, oth1, rp, rb, eq, 0)
        fill_p(own2, oth2, rp, rb, eq, 1)

    own1, oth1, own2, oth2 = kernel_call(
        pack_body,
        [((chips, msg, B), BF)] * 4,
        [],
        [region_blocks, equivalents, innovations],
        scratch=[
            pltpu.VMEM((rows, cols), F32),
            pltpu.VMEM((rows, cols), F32),
            pltpu.SMEM(region_blocks.shape, jnp.int32),
            pltpu.SemaphoreType.DMA((3,)),
        ],
        name="pack",
        array_spec=HBM_SPEC,
        vmem=52 * 1024 * 1024,
    )
    core_pairs = [(i, i ^ 1) for i in range(n)]

    def swap_core(x):
        return lax.ppermute(x, "mem", core_pairs)

    def z_exchange(parts, order):
        got = list(parts)
        for k in order:
            got[k] = lax.ppermute(parts[k], "mem", [(i, i ^ (2 * k)) for i in range(n)])
        return got

    far_first = list(range(1, chips))[::-1]
    top = chips // 2

    def z_send(x, k):
        return lax.ppermute(x, "mem", [(i, i ^ (2 * k)) for i in range(n)])


    def join_body(own, oth, *outs):
        for k in range(chips):
            out = outs[k]
            out[0:rp, :] = own[k, rp:step, :]
            out[rp:step, :] = oth[k, rp:step, :]
            out[step : step + rp, :] = own[k, 0:rp, :]
            out[step + rp : 2 * step, :] = oth[k, 0:rp, :]
            out[2 * step :, :] = own[k, step:msg, :] + oth[k, step:msg, :]

    def join(own, oth, name, after=()):
        return kernel_call(
            join_body, [((msg + step, B), BF)] * chips, [], [own, oth], name=name, after=after
        )

    m1_got = z_exchange(join(own1, swap_core(oth1), "join_first"), far_first)
    coef = chebyshev(eig_low[0], eig_high[0], B)
    m2_parts = join(
        own2, swap_core(oth2), "join_second", after=[taper_index, pair_mask, region_blocks, coef]
    )
    m2_got = z_exchange(m2_parts, far_first)

    def corrected(pieces):
        mean = sum(m for _, m in pieces) * (1.0 / n)
        out = []
        for x, m in pieces:
            x = x.astype(F32) + (m - mean) * inv_scale
            if rp > rows:
                x = jnp.where(lax.broadcasted_iota(jnp.int32, (rp, B), 0) < rows, x, 0.0)
            out.append(x.astype(BF))
        return out

    odd = range(1, n_lat - 1, 2)
    pair_list = [(i, i ^ 1) for i in range(n_lat)]
    skew_list = [(i, i + 1) for i in odd] + [(i + 1, i) for i in odd]
    hop1_list = [(i, i + 2) for i in odd] + [(i + 1, i - 1) for i in odd]
    hop2_list = [(i + 2, i + 1) for i in odd] + [(i - 1, i) for i in odd]

    def lat_exchange(both, low, high, after=(), low_after=()):
        relay = lax.ppermute(high, "lat", hop1_list)
        pair = lax.ppermute(both, "lat", pair_list)
        skew_low = lax.ppermute(gate(low, low_after) if low_after else low, "lat", skew_list)
        skew_high = lax.ppermute(gate(relay, after) if after else relay, "lat", hop2_list)
        return pair, skew_low, skew_high, relay

    block_out = ((mp, B), BF)
    half_out = ((half, B), BF)

    def group_rows(part):
        tail = part[2 * step :, :].astype(F32)
        return [
            (part[j * rp : (j + 1) * rp, :], jnp.sum(tail[3 * j : 3 * j + 3, :], axis=0, keepdims=True))
            for j in range(2)
        ]

    def owner_body(*refs):
        parts, (both, low, high) = refs[:chips], refs[chips:]

        def put(lo, i, value):
            both[lo * 2 + i * rp : lo * 2 + (i + 1) * rp, :] = value
            out, at = (low, lo + i * rp) if i < chips else (high, lo + (i - chips) * rp)
            out[at : at + rp, :] = value

        for i in range(n):
            at = step + (i % 2) * rp
            put(half, i, parts[i // 2][at : at + rp, :])
        for i, x in enumerate(corrected([g for part in parts for g in group_rows(part)])):
            put(0, i, x)

    both_out = ((2 * mp, B), BF)
    first, first_low, first_high = kernel_call(
        owner_body, [both_out, block_out, block_out], [], m1_got, name="owner_first", after=[m2_parts[0]]
    )
    pair, skew_low, skew_high, relay = lat_exchange(first, first_low, first_high, after=[m2_got[1]])

    var_row = obs_var.reshape(1, cols)

    def whole(low, high):
        return jnp.concatenate([low[...], high[...]], axis=0)

    mat = ((B, B), BF)
    field = ((mp, B), F32)
    half_field = ((half, B), F32)

    def tiles_body(rb, ti, tt, first_ref, t_first, t_second, t_pair, t_skew, p1t):
        me, band = lax.axis_index("mem"), lax.axis_index("lat")
        first = region_start(rb, band, me)
        second = jnp.minimum(first + 1, nb - 1)
        below = jnp.maximum(band - 1, 0)
        even = lax.rem(band, 2) == 0
        for block, out in ((first, t_first), (second, t_second)):
            tile = tt[ti[band, block, 0]].astype(F32)
            out[...] = 0.5 * (tile + tile.T)
        up = tt[ti[band, first, 2]].astype(F32)
        down = tt[ti[below, region_start(rb, below, me), 2]].astype(F32).T
        t_pair[...] = jnp.where(even, up, down).astype(BF)
        t_skew[...] = jnp.where(even, down, up).astype(BF)
        p1t[...] = first_ref[0:mp, :].astype(F32).T.astype(BF)

    square = ((B, B), F32)
    t_first, t_second, t_pair, t_skew, p1t = kernel_call(
        tiles_body,
        [square, square, mat, mat, ((B, mp), BF)],
        [region_blocks, taper_index],
        [taper_tiles, first],
        name="tiles",
    )

    def first_body(first_ref, t_ref, p1t_ref, s1, z1):
        s1[...] = (t_ref[...] * dot_nn(p1t_ref[...], first_ref[0:mp, :])).astype(BF)
        z1[...] = dot_nn(first_ref[mp:, :], s1[...])

    s1, z1 = kernel_call(
        first_body, [mat, field], [], [first, t_first, p1t], name="first_cov"
    )

    def pair_body(t_ref, p1t_ref, pair_ref, z1_ref, qp, z1):
        qp[...] = (t_ref[...].astype(F32) * dot_nn(p1t_ref[...], pair_ref[0:mp, :])).astype(BF)
        z1[...] = z1_ref[...] + dot_nt(pair_ref[mp:, :], qp[...])

    qp, z1 = kernel_call(
        pair_body,
        [mat, field],
        [],
        [t_pair, p1t, pair, z1],
        name="pair_cov",
    )

    def east_body(rb, pm, ti, tt, p1t_ref, *refs):
        parts, (z1_ref, ce, z1, p2, r2) = refs[:chips], refs[chips:]
        me, band = lax.axis_index("mem"), lax.axis_index("lat")
        first = region_start(rb, band, me)
        for k in range(chips):
            r2[k * step : (k + 1) * step, :] = parts[k][step : 2 * step, :]
        for i, x in enumerate(corrected([g for part in parts for g in group_rows(part)])):
            p2[i * rp : (i + 1) * rp, :] = x
        active = ((rb[band, me] > 1) & (pm[band, first] == 1)).astype(F32)
        tile_east = tt[ti[band, first, 1]].astype(F32) * active
        ce[...] = (tile_east * dot_nn(p1t_ref[...], p2[...])).astype(BF)
        z1[...] = z1_ref[...] + dot_nt(r2[...], ce[...])

    ce, z1, p2, r2 = kernel_call(
        east_body,
        [mat, field, block_out, block_out],
        [region_blocks, pair_mask, taper_index],
        [taper_tiles, p1t, *m2_got, z1],
        name="east_cov",
    )

    def skew_body(t_ref, p1t_ref, sl, sh, z1_ref, qs, z1):
        skew_p = jnp.concatenate([sl[0:half, :], sh[0:half, :]], axis=0)
        skew_r = jnp.concatenate([sl[half:, :], sh[half:, :]], axis=0)
        qs[...] = (t_ref[...].astype(F32) * dot_nn(p1t_ref[...], skew_p)).astype(BF)
        z1[...] = z1_ref[...] + dot_nt(skew_r, qs[...])

    qs, z1 = kernel_call(
        skew_body,
        [mat, field],
        [],
        [t_skew, p1t, skew_low, skew_high, z1],
        name="skew_cov",
    )

    def direction_body(rb, coef, var, first_ref, z1_ref, d1, d1l, d1h, t1):
        me, band = lax.axis_index("mem"), lax.axis_index("lat")
        first = region_start(rb, band, me)
        inv_c, keep1, gain1, keep2, gain2 = coefficients(coef)
        var1 = var[:, block_cols(first, B)]
        prod = z1_ref[...]
        r1f = first_ref[mp:, :].astype(F32)
        d0 = r1f * inv_c
        res = r1f - (var1 * d0 + prod * inv_c)
        d = keep1 * d0 + gain1 * res
        db = d.astype(BF)
        d1[...] = db
        d1l[...] = db[0:half, :]
        d1h[...] = db[half:mp, :]
        t1[...] = (1.0 + keep2) * d + gain2 * (res - var1 * d)

    d1, d1_low, d1_high, t1 = kernel_call(
        direction_body,
        [block_out, half_out, half_out, field],
        [region_blocks],
        [coef, var_row, first, z1],
        name="direction_first",
    )
    def inner_body(
        rb, coef, t_ref, var, p2_ref, r2_ref, first_ref, s1_ref, ce_ref, d1_ref, t1_ref, w1, *outs
    ):
        me, band = lax.axis_index("mem"), lax.axis_index("lat")
        second = jnp.minimum(region_start(rb, band, me) + 1, nb - 1)
        inv_c, keep1, gain1, keep2, gain2 = coefficients(coef)
        d1v, r2v, cev = d1_ref[...], r2_ref[...], ce_ref[...]
        s2 = (t_ref[...] * dot_tn(p2_ref[...], p2_ref[...])).astype(BF)
        prod = dot_nn(r2v, s2) + dot_nn(first_ref[mp:, :], cev)
        var2 = var[:, block_cols(second, B)]
        r2f = r2v.astype(F32)
        d0 = r2f * inv_c
        res = r2f - (var2 * d0 + prod * inv_c)
        d2 = keep1 * d0 + gain1 * res
        d2b = d2.astype(BF)
        w1[...] = t1_ref[...] - gain2 * (dot_nn(d1v, s1_ref[...]) + dot_nt(d2b, cev))
        sol = (1.0 + keep2) * d2 + gain2 * (res - var2 * d2 - dot_nn(d2b, s2) - dot_nn(d1v, cev))
        outs[0][...] = sol[0:half, :].astype(BF)
        for k in range(top, chips):
            outs[k - top + 1][...] = sol[k * step : (k + 1) * step, :].astype(BF)

    w1, sol2_near, *sol2_far = kernel_call(
        inner_body,
        [field, half_out] + [((step, B), BF)] * top,
        [region_blocks],
        [coef, t_second, var_row, p2, r2, first, s1, ce, d1, t1],
        name="inner_step",
    )
    d1_pair, d1_skew_low, d1_skew_high, d1_relay = lat_exchange(d1, d1_low, d1_high, low_after=[w1], after=[w1])
    sol2_far = [z_send(gate(x, [d1_relay]), k + top) for k, x in list(enumerate(sol2_far))[::-1]][::-1]

    def outer_body(coef, qp_ref, qs_ref, dp, dsl, dsh, w1_ref, near_ref, *outs):
        gain2 = coefficients(coef)[4]
        prod = dot_nt(dp[...], qp_ref[...]) + dot_nt(whole(dsl, dsh), qs_ref[...])
        sol = w1_ref[...] - gain2 * prod
        for i in range(n):
            rows_i = slice(i * rp, (i + 1) * rp)
            if i < chips:
                outs[i][0:rp, :] = sol[rows_i, :].astype(BF)
                outs[i][rp:step, :] = near_ref[rows_i, :]
            else:
                at = (i % 2) * rp
                outs[chips + (i - chips) // 2][at : at + rp, :] = sol[rows_i, :].astype(BF)

    sol1 = kernel_call(
        outer_body,
        [((step, B), BF)] * (chips + top),
        [],
        [coef, qp, qs, d1_pair, d1_skew_low, d1_skew_high, w1, sol2_near],
        name="outer_step",
    )
    sol1_far = [z_send(x, k + top) for k, x in list(enumerate(sol1[chips:]))[::-1]][::-1]
    sol1_near = [
        x if i == 0 else lax.ppermute(x, "mem", [(q, q ^ i) for q in range(n)])
        for i, x in enumerate(sol1[:chips])
    ]

    def peer_body(*refs):
        for k in range(2 * top):
            refs[2 * top][k] = refs[k][rp:step, :]

    (peer,) = kernel_call(
        peer_body, [((2 * top, rp, B), BF)], [], [*sol1_far, *sol2_far], name="peer_rows", after=sol1_near[1:]
    )
    peer = swap_core(peer)

    def unpack_body(rb, coef, inn, *refs):
        near, far1, far2 = refs[:chips], refs[chips : chips + top], refs[chips + top : 2 * chips]
        peer, out = refs[2 * chips :]
        me, band = lax.axis_index("mem"), lax.axis_index("lat")
        inv_c = coefficients(coef)[0]

        def pieces(i):
            k = i // 2 - top
            if k < 0:
                return near[i][0:rows, :], near[i][rp : rp + rows, :]
            if i % 2:
                return peer[k, 0:rows, :], peer[top + k, 0:rows, :]
            return far1[k][0:rows, :], far2[k][0:rows, :]

        for i in range(n):
            owner = me ^ i
            first = region_start(rb, band, owner)
            at = block_cols(first, B)
            out[:, at] = inn[:, at] * inv_c + pieces(i)[0].astype(F32)
            second = jnp.minimum(first + 1, nb - 1)

            @pl.when(rb[band, owner] > 1)
            def _(i=i, second=second):
                at2 = block_cols(second, B)
                out[:, at2] = inn[:, at2] * inv_c + pieces(i)[1].astype(F32)

    (out,) = kernel_call(
        unpack_body,
        [((rows, cols), F32)],
        [region_blocks],
        [coef, innovations, *sol1_near, *sol1_far, *sol2_far, peer],
        name="unpack",
    )
    return out


def solution(mesh):
    return jax.shard_map(
        on_device,
        mesh=mesh,
        in_specs=(P("mem", "lat"), P("mem", "lat"), P("lat"), P(), P(), P(), P(), P(), P()),
        out_specs=P("mem", "lat"),
        check_vma=False,
    )
```

```python
import math

import jax
import jax.numpy as jnp
from jax import lax
from jax.experimental import pallas as pl
from jax.experimental.pallas import tpu as pltpu
from jax.sharding import PartitionSpec as P

BF = jnp.bfloat16
F32 = jnp.float32
VMEM_LIMIT = 12 * 1024 * 1024

SMEM_SPEC = pl.BlockSpec(memory_space=pltpu.SMEM)
VMEM_SPEC = pl.BlockSpec(memory_space=pltpu.VMEM)
ANY_SPEC = pl.BlockSpec(memory_space=pl.ANY)
HBM_SPEC = pl.BlockSpec(memory_space=pltpu.HBM)


def kernel_call(body, outs, scalars, arrays, scratch=(), name=None, array_spec=VMEM_SPEC, after=(), vmem=VMEM_LIMIT):
    used, unread = len(scalars) + len(arrays), len(after)
    moved = sum(a.size * a.dtype.itemsize for a in arrays)
    moved += sum(jnp.dtype(d).itemsize * math.prod(s) for s, d in outs)

    def run(*refs):
        body(*refs[:used], *refs[used + unread :])

    return pl.pallas_call(
        run,
        out_shape=tuple(jax.ShapeDtypeStruct(s, d) for s, d in outs),
        in_specs=[SMEM_SPEC] * len(scalars) + [array_spec] * len(arrays) + [ANY_SPEC] * unread,
        out_specs=tuple(VMEM_SPEC for _ in outs),
        scratch_shapes=list(scratch),
        compiler_params=pltpu.CompilerParams(vmem_limit_bytes=vmem),
        cost_estimate=pl.CostEstimate(flops=3 * 10**9, bytes_accessed=3 * 10**7, transcendentals=0),
        name=name,
    )(*scalars, *arrays, *after)


def gate(x, after):
    def nothing(*refs):
        del refs

    return pl.pallas_call(
        nothing,
        out_shape=jax.ShapeDtypeStruct(x.shape, x.dtype),
        in_specs=[ANY_SPEC] * (1 + len(after)),
        out_specs=ANY_SPEC,
        input_output_aliases={0: 0},
        compiler_params=pltpu.CompilerParams(vmem_limit_bytes=1024 * 1024),
        name="gate",
    )(x, *after)


def dot_nn(a, b):
    return lax.dot_general(a, b, (((1,), (0,)), ((), ())), preferred_element_type=F32)


def dot_nt(a, b):
    return lax.dot_general(a, b, (((1,), (1,)), ((), ())), preferred_element_type=F32)


def dot_tn(a, b):
    return lax.dot_general(a, b, (((0,), (0,)), ((), ())), preferred_element_type=F32)


def region_start(rb, band, m):
    return lax.fori_loop(0, m, lambda i, acc: acc + rb[band, i], jnp.int32(0))


def block_cols(block, width):
    return pl.ds(pl.multiple_of(block * width, width), width)


def chebyshev(low, high, width):
    low = jnp.broadcast_to(low, (8, width))
    high = jnp.broadcast_to(high, (8, width))
    centre = 0.5 * (high + low)
    half = 0.5 * (high - low)
    s = centre / half
    q0 = 1.0 / s
    q1 = 1.0 / (2.0 * s - q0)
    q2 = 1.0 / (2.0 * s - q1)
    row = lax.broadcasted_iota(jnp.int32, (8, width), 0)
    out = 1.0 / centre
    for i, value in enumerate((q1 * q0, 2.0 * q1 / half, q2 * q1, 2.0 * q2 / half)):
        out = jnp.where(row == i + 1, value, out)
    return out


def coefficients(coef):
    return [coef[i : i + 1, :] for i in range(5)]


def on_device(
    equivalents,
    innovations,
    obs_var,
    taper_tiles,
    region_blocks,
    pair_mask,
    taper_index,
    eig_low,
    eig_high,
):
    n = lax.axis_size("mem")
    n_lat = lax.axis_size("lat")
    chips = n // 2
    rows, cols = equivalents.shape
    B = taper_tiles.shape[1]
    nb = cols // B
    members = rows * n
    inv_scale = (members - 1) ** (-0.5)
    rp = -(-rows // 16) * 16
    mp = rp * n
    half = mp // 2

    def put_rows(ref_set, lo, value):
        ref_set(slice(lo, lo + rows), value)
        if rp > rows:
            ref_set(slice(lo + rows, lo + rp), jnp.zeros((rp - rows, B), value.dtype))

    tail_rows = 8
    msg = 2 * rp + tail_rows
    step = 2 * rp

    def mean_rows(x, offset):
        mean = jnp.sum(x, axis=0, keepdims=True) * (1.0 / rows)
        high = mean.astype(BF).astype(F32)
        mid = (mean - high).astype(BF).astype(F32)
        row = lax.broadcasted_iota(jnp.int32, (tail_rows, B), 0)
        tail = jnp.where(row == offset + 2, mean - high - mid, 0.0)
        tail = jnp.where(row == offset + 1, mid, tail)
        tail = jnp.where(row == offset, high, tail)
        return mean, tail.astype(BF)

    def owner_starts(rb):
        me, band = lax.axis_index("mem"), lax.axis_index("lat")
        prefix, starts = jnp.int32(0), [jnp.int32(0)] * n
        for m in range(n):
            starts = [jnp.where((me ^ i) == m, prefix, s) for i, s in enumerate(starts)]
            prefix = prefix + rb[band, m]
        return starts

    def blocks(starts, extra):
        return [block_cols(jnp.minimum(first + extra, nb - 1), B) for first in starts]

    def fill_p(own, oth, at_row, starts, eq, extra):
        for i, at in enumerate(blocks(starts, extra)):
            k, j = i // 2, i % 2
            out = oth if j else own
            x = eq[:, at]
            mean, tail = mean_rows(x, 3 * j)
            put = lambda s, v: out.__setitem__((k, s), v)
            put_rows(put, at_row, ((x - mean) * inv_scale).astype(BF))
            out[k, step:msg, :] = tail

    def fill_r(own, oth, starts, inn, extra):
        for i, at in enumerate(blocks(starts, extra)):
            out = oth if i % 2 else own
            put_rows(lambda s, v: out.__setitem__((i // 2, s), v), 0, inn[:, at].astype(BF))

    def pack_body(rb_hbm, eq_hbm, inn_hbm, own1, oth1, own2, oth2, eq, inn, rb, sems):
        copies = [
            pltpu.make_async_copy(src, dst, sems.at[i])
            for i, (src, dst) in enumerate(((rb_hbm, rb), (inn_hbm, inn), (eq_hbm, eq)))
        ]
        for copy in copies:
            copy.start()
        copies[0].wait()
        starts = owner_starts(rb)
        copies[1].wait()
        fill_r(own1, oth1, starts, inn, 0)
        fill_r(own2, oth2, starts, inn, 1)
        copies[2].wait()
        fill_p(own1, oth1, rp, starts, eq, 0)
        fill_p(own2, oth2, rp, starts, eq, 1)

    own1, oth1, own2, oth2 = kernel_call(
        pack_body,
        [((chips, msg, B), BF)] * 4,
        [],
        [region_blocks, equivalents, innovations],
        scratch=[
            pltpu.VMEM((rows, cols), F32),
            pltpu.VMEM((rows, cols), F32),
            pltpu.SMEM(region_blocks.shape, jnp.int32),
            pltpu.SemaphoreType.DMA((3,)),
        ],
        name="pack",
        array_spec=HBM_SPEC,
        vmem=52 * 1024 * 1024,
    )
    core_pairs = [(i, i ^ 1) for i in range(n)]

    def swap_core(x):
        return lax.ppermute(x, "mem", core_pairs)

    def z_exchange(parts, order):
        got = list(parts)
        for k in order:
            got[k] = lax.ppermute(parts[k], "mem", [(i, i ^ (2 * k)) for i in range(n)])
        return got

    far_first = list(range(1, chips))[::-1]
    top = chips // 2

    def z_send(x, k):
        return lax.ppermute(x, "mem", [(i, i ^ (2 * k)) for i in range(n)])


    def join_body(own, oth, *outs):
        for k in range(chips):
            out = outs[k]
            out[0:rp, :] = own[k, rp:step, :]
            out[rp:step, :] = oth[k, rp:step, :]
            out[step : step + rp, :] = own[k, 0:rp, :]
            out[step + rp : 2 * step, :] = oth[k, 0:rp, :]
            out[2 * step :, :] = own[k, step:msg, :] + oth[k, step:msg, :]

    def join(own, oth, name, after=()):
        return kernel_call(
            join_body, [((msg + step, B), BF)] * chips, [], [own, oth], name=name, after=after
        )

    m1_got = z_exchange(join(own1, swap_core(oth1), "join_first"), far_first)
    coef = chebyshev(eig_low[0], eig_high[0], B)
    m2_parts = join(
        own2, swap_core(oth2), "join_second", after=[taper_index, pair_mask, region_blocks, coef]
    )
    m2_got = z_exchange(m2_parts, far_first)

    def corrected(pieces):
        mean = sum(m for _, m in pieces) * (1.0 / n)
        out = []
        for x, m in pieces:
            x = x.astype(F32) + (m - mean) * inv_scale
            if rp > rows:
                x = jnp.where(lax.broadcasted_iota(jnp.int32, (rp, B), 0) < rows, x, 0.0)
            out.append(x.astype(BF))
        return out

    odd = range(1, n_lat - 1, 2)
    pair_list = [(i, i ^ 1) for i in range(n_lat)]
    skew_list = [(i, i + 1) for i in odd] + [(i + 1, i) for i in odd]
    hop1_list = [(i, i + 2) for i in odd] + [(i + 1, i - 1) for i in odd]
    hop2_list = [(i + 2, i + 1) for i in odd] + [(i - 1, i) for i in odd]

    def lat_exchange(both, low, high, after=(), low_after=()):
        relay = lax.ppermute(high, "lat", hop1_list)
        pair = lax.ppermute(both, "lat", pair_list)
        skew_low = lax.ppermute(gate(low, low_after) if low_after else low, "lat", skew_list)
        skew_high = lax.ppermute(gate(relay, after) if after else relay, "lat", hop2_list)
        return pair, skew_low, skew_high, relay

    block_out = ((mp, B), BF)
    half_out = ((half, B), BF)

    def group_rows(part):
        tail = part[2 * step :, :].astype(F32)
        return [
            (part[j * rp : (j + 1) * rp, :], jnp.sum(tail[3 * j : 3 * j + 3, :], axis=0, keepdims=True))
            for j in range(2)
        ]

    def owner_body(*refs):
        parts, (both, low, high) = refs[:chips], refs[chips:]

        def put(lo, i, value):
            both[lo * 2 + i * rp : lo * 2 + (i + 1) * rp, :] = value
            out, at = (low, lo + i * rp) if i < chips else (high, lo + (i - chips) * rp)
            out[at : at + rp, :] = value

        for i in range(n):
            at = step + (i % 2) * rp
            put(half, i, parts[i // 2][at : at + rp, :])
        for i, x in enumerate(corrected([g for part in parts for g in group_rows(part)])):
            put(0, i, x)

    both_out = ((2 * mp, B), BF)
    first, first_low, first_high = kernel_call(
        owner_body, [both_out, block_out, block_out], [], m1_got, name="owner_first", after=[m2_parts[0]]
    )
    pair, skew_low, skew_high, relay = lat_exchange(first, first_low, first_high, after=[m2_got[1]])

    var_row = obs_var.reshape(1, cols)

    def whole(low, high):
        return jnp.concatenate([low[...], high[...]], axis=0)

    mat = ((B, B), BF)
    field = ((mp, B), F32)
    half_field = ((half, B), F32)

    def tiles_body(rb, ti, tt, first_ref, t_first, t_second, t_pair, t_skew, p1t):
        me, band = lax.axis_index("mem"), lax.axis_index("lat")
        first = region_start(rb, band, me)
        second = jnp.minimum(first + 1, nb - 1)
        below = jnp.maximum(band - 1, 0)
        even = lax.rem(band, 2) == 0
        for block, out in ((first, t_first), (second, t_second)):
            tile = tt[ti[band, block, 0]].astype(F32)
            out[...] = 0.5 * (tile + tile.T)
        up = tt[ti[band, first, 2]].astype(F32)
        down = tt[ti[below, region_start(rb, below, me), 2]].astype(F32).T
        t_pair[...] = jnp.where(even, up, down).astype(BF)
        t_skew[...] = jnp.where(even, down, up).astype(BF)
        p1t[...] = first_ref[0:mp, :].astype(F32).T.astype(BF)

    square = ((B, B), F32)
    t_first, t_second, t_pair, t_skew, p1t = kernel_call(
        tiles_body,
        [square, square, mat, mat, ((B, mp), BF)],
        [region_blocks, taper_index],
        [taper_tiles, first],
        name="tiles",
    )

    def first_body(first_ref, t_ref, p1t_ref, s1, z1):
        s1[...] = (t_ref[...] * dot_nn(p1t_ref[...], first_ref[0:mp, :])).astype(BF)
        z1[...] = dot_nn(first_ref[mp:, :], s1[...])

    s1, z1 = kernel_call(
        first_body, [mat, field], [], [first, t_first, p1t], name="first_cov"
    )

    def pair_body(t_ref, p1t_ref, pair_ref, z1_ref, qp, z1):
        qp[...] = (t_ref[...].astype(F32) * dot_nn(p1t_ref[...], pair_ref[0:mp, :])).astype(BF)
        z1[...] = z1_ref[...] + dot_nt(pair_ref[mp:, :], qp[...])

    qp, z1 = kernel_call(
        pair_body,
        [mat, field],
        [],
        [t_pair, p1t, pair, z1],
        name="pair_cov",
    )

    def east_body(rb, pm, ti, tt, p1t_ref, *refs):
        parts, (z1_ref, ce, z1, p2, r2) = refs[:chips], refs[chips:]
        me, band = lax.axis_index("mem"), lax.axis_index("lat")
        first = region_start(rb, band, me)
        for k in range(chips):
            r2[k * step : (k + 1) * step, :] = parts[k][step : 2 * step, :]
        for i, x in enumerate(corrected([g for part in parts for g in group_rows(part)])):
            p2[i * rp : (i + 1) * rp, :] = x
        active = ((rb[band, me] > 1) & (pm[band, first] == 1)).astype(F32)
        tile_east = tt[ti[band, first, 1]].astype(F32) * active
        ce[...] = (tile_east * dot_nn(p1t_ref[...], p2[...])).astype(BF)
        z1[...] = z1_ref[...] + dot_nt(r2[...], ce[...])

    ce, z1, p2, r2 = kernel_call(
        east_body,
        [mat, field, block_out, block_out],
        [region_blocks, pair_mask, taper_index],
        [taper_tiles, p1t, *m2_got, z1],
        name="east_cov",
    )

    def skew_body(t_ref, p1t_ref, sl, sh, z1_ref, qs, z1):
        skew_p = jnp.concatenate([sl[0:half, :], sh[0:half, :]], axis=0)
        skew_r = jnp.concatenate([sl[half:, :], sh[half:, :]], axis=0)
        qs[...] = (t_ref[...].astype(F32) * dot_nn(p1t_ref[...], skew_p)).astype(BF)
        z1[...] = z1_ref[...] + dot_nt(skew_r, qs[...])

    qs, z1 = kernel_call(
        skew_body,
        [mat, field],
        [],
        [t_skew, p1t, skew_low, skew_high, z1],
        name="skew_cov",
    )

    def direction_body(rb, coef, var, first_ref, z1_ref, d1, d1l, d1h, t1):
        me, band = lax.axis_index("mem"), lax.axis_index("lat")
        first = region_start(rb, band, me)
        inv_c, keep1, gain1, keep2, gain2 = coefficients(coef)
        var1 = var[:, block_cols(first, B)]
        prod = z1_ref[...]
        r1f = first_ref[mp:, :].astype(F32)
        d0 = r1f * inv_c
        res = r1f - (var1 * d0 + prod * inv_c)
        d = keep1 * d0 + gain1 * res
        db = d.astype(BF)
        d1[...] = db
        d1l[...] = db[0:half, :]
        d1h[...] = db[half:mp, :]
        t1[...] = (1.0 + keep2) * d + gain2 * (res - var1 * d)

    d1, d1_low, d1_high, t1 = kernel_call(
        direction_body,
        [block_out, half_out, half_out, field],
        [region_blocks],
        [coef, var_row, first, z1],
        name="direction_first",
    )
    def inner_body(
        rb, coef, t_ref, var, p2_ref, r2_ref, first_ref, s1_ref, ce_ref, d1_ref, t1_ref, w1, *outs
    ):
        me, band = lax.axis_index("mem"), lax.axis_index("lat")
        second = jnp.minimum(region_start(rb, band, me) + 1, nb - 1)
        inv_c, keep1, gain1, keep2, gain2 = coefficients(coef)
        d1v, r2v, cev = d1_ref[...], r2_ref[...], ce_ref[...]
        s2 = (t_ref[...] * dot_tn(p2_ref[...], p2_ref[...])).astype(BF)
        prod = dot_nn(r2v, s2) + dot_nn(first_ref[mp:, :], cev)
        var2 = var[:, block_cols(second, B)]
        r2f = r2v.astype(F32)
        d0 = r2f * inv_c
        res = r2f - (var2 * d0 + prod * inv_c)
        d2 = keep1 * d0 + gain1 * res
        d2b = d2.astype(BF)
        w1[...] = t1_ref[...] - gain2 * (dot_nn(d1v, s1_ref[...]) + dot_nt(d2b, cev))
        sol = (1.0 + keep2) * d2 + gain2 * (res - var2 * d2 - dot_nn(d2b, s2) - dot_nn(d1v, cev))
        outs[0][...] = sol[0:half, :].astype(BF)
        for k in range(top, chips):
            outs[k - top + 1][...] = sol[k * step : (k + 1) * step, :].astype(BF)

    w1, sol2_near, *sol2_far = kernel_call(
        inner_body,
        [field, half_out] + [((step, B), BF)] * top,
        [region_blocks],
        [coef, t_second, var_row, p2, r2, first, s1, ce, d1, t1],
        name="inner_step",
    )
    d1_pair, d1_skew_low, d1_skew_high, d1_relay = lat_exchange(d1, d1_low, d1_high, low_after=[w1], after=[w1])
    sol2_far = [z_send(gate(x, [d1_relay]), k + top) for k, x in list(enumerate(sol2_far))[::-1]][::-1]

    def outer_body(coef, qp_ref, qs_ref, dp, dsl, dsh, w1_ref, near_ref, *outs):
        gain2 = coefficients(coef)[4]
        prod = dot_nt(dp[...], qp_ref[...]) + dot_nt(whole(dsl, dsh), qs_ref[...])
        sol = w1_ref[...] - gain2 * prod
        for i in range(n):
            rows_i = slice(i * rp, (i + 1) * rp)
            if i < chips:
                outs[i][0:rp, :] = sol[rows_i, :].astype(BF)
                outs[i][rp:step, :] = near_ref[rows_i, :]
            else:
                at = (i % 2) * rp
                outs[chips + (i - chips) // 2][at : at + rp, :] = sol[rows_i, :].astype(BF)

    sol1 = kernel_call(
        outer_body,
        [((step, B), BF)] * (chips + top),
        [],
        [coef, qp, qs, d1_pair, d1_skew_low, d1_skew_high, w1, sol2_near],
        name="outer_step",
    )
    sol1_far = [z_send(x, k + top) for k, x in list(enumerate(sol1[chips:]))[::-1]][::-1]
    sol1_near = [
        x if i < 2 else lax.ppermute(x, "mem", [(q, q ^ i) for q in range(n)])
        for i, x in enumerate(sol1[:chips])
    ]

    def peer_body(*refs):
        out = refs[-1]
        for k in range(2 * top):
            out[k] = refs[k][rp:step, :]
        out[2 * top] = refs[2 * top][0:rp, :]
        out[2 * top + 1] = refs[2 * top][rp:step, :]

    (peer,) = kernel_call(
        peer_body,
        [((2 * top + 2, rp, B), BF)],
        [],
        [*sol1_far, *sol2_far, sol1_near[1]],
        name="peer_rows",
        after=sol1_near[2:],
    )
    peer = swap_core(peer)

    def unpack_body(rb, coef, inn, *refs):
        near, far1, far2 = refs[:chips], refs[chips : chips + top], refs[chips + top : 2 * chips]
        peer, out, buf, sems = refs[2 * chips :]
        me, band = lax.axis_index("mem"), lax.axis_index("lat")
        inv_c = coefficients(coef)[0]

        def pieces(i):
            k = i // 2 - top
            if i == 1:
                return peer[2 * top, 0:rows, :], peer[2 * top + 1, 0:rows, :]
            if k < 0:
                return near[i][0:rows, :], near[i][rp : rp + rows, :]
            if i % 2:
                return peer[k, 0:rows, :], peer[top + k, 0:rows, :]
            return far1[k][0:rows, :], far2[k][0:rows, :]

        waits, starts = [], owner_starts(rb)

        def write(at, number, value):
            buf[number] = inn[:, at] * inv_c + value.astype(F32)
            copy = pltpu.make_async_copy(buf.at[number], out.at[:, at], sems.at[number])
            copy.start()
            return copy

        for i in range(n):
            owner = me ^ i
            first = starts[i]
            waits.append(write(block_cols(first, B), 2 * i, pieces(i)[0]))
            at = block_cols(jnp.minimum(first + 1, nb - 1), B)

            @pl.when(rb[band, owner] > 1)
            def _(i=i, at=at):
                write(at, 2 * i + 1, pieces(i)[1])

        for i in range(n):
            waits[i].wait()
            owner = me ^ i
            at = block_cols(jnp.minimum(starts[i] + 1, nb - 1), B)

            @pl.when(rb[band, owner] > 1)
            def _(i=i, at=at):
                number = 2 * i + 1
                pltpu.make_async_copy(buf.at[number], out.at[:, at], sems.at[number]).wait()

    arrays = [coef, innovations, *sol1_near, *sol1_far, *sol2_far, peer]
    return pl.pallas_call(
        unpack_body,
        out_shape=jax.ShapeDtypeStruct((rows, cols), F32),
        in_specs=[SMEM_SPEC] + [VMEM_SPEC] * len(arrays),
        out_specs=HBM_SPEC,
        scratch_shapes=[pltpu.VMEM((2 * n, rows, B), F32), pltpu.SemaphoreType.DMA((2 * n,))],
        compiler_params=pltpu.CompilerParams(vmem_limit_bytes=VMEM_LIMIT),
        cost_estimate=pl.CostEstimate(flops=3 * 10**9, bytes_accessed=3 * 10**7, transcendentals=0),
        name="unpack",
    )(region_blocks, *arrays)


def solution(mesh):
    return jax.shard_map(
        on_device,
        mesh=mesh,
        in_specs=(P("mem", "lat"), P("mem", "lat"), P("lat"), P(), P(), P(), P(), P(), P()),
        out_specs=P("mem", "lat"),
        check_vma=False,
    )
```
